32 devices in a mesh: dp: 8 (over z, y), tensor: 4 (over x, core).
Axes of the slice: x: 2, y: 2, z: 4, core: 2. Of those that a mesh axis runs over, the one named last changes fastest.
Arguments:
- tokens: bfloat16 [4096, 4096], P(('dp', 'tensor')), may hold values from -6 to 6
- weight: bfloat16 [4096, 4096], P('tensor', 'dp'), may hold values from -0.09375 to 0.09375
Outputs:
- projected: bfloat16 [4096, 4096], P('dp', 'tensor')
The draws below stay inside these ranges and needn't reach their ends.
All inputs are finite; a program needn't handle non-finite values.
Results may differ from the reference program's by a relative error of at most 0.0057.
Values may be sent and summed in bfloat16 or wider, within the bound.
No kernel may reach another device: no remote copies, remote signals or barrier semaphores. Data moves between devices by JAX's collectives and lax.ppermute only.
A program may use at most 64 MiB of HBM per device.

```python
import jax
import jax.numpy as jnp

D = 4096
TOKENS = 4096


def levels(rng, shape, cuts, low, high):
    level = 1.0
    for axis_at, parts in cuts:
        steps = jax.random.uniform(jax.random.fold_in(jax.random.fold_in(rng, 6), axis_at), (parts,), jnp.float32, low / len(cuts), high / len(cuts))
        level = level * jnp.repeat(jnp.exp(steps), shape[axis_at] // parts).reshape((-1,) + (1,) * (len(shape) - 1 - axis_at))
    return level


def gaussian(key, shape, width, most, shards=(), dtype=jnp.bfloat16):
    values = width * jax.random.normal(key, shape, jnp.float32)
    if shards:
        values = values * levels(key, shape, shards, -0.22, 0.18)
    return jnp.clip(values, -most, most).astype(dtype)


def setup_inputs(seed: int = 0) -> dict:
    key_list = jax.random.split(jax.random.key(seed), 3)
    tokens = gaussian(key_list[0], (TOKENS, D), 1.0, 6.0, ((0, 32),))
    weight = gaussian(key_list[1], (D, D), D ** -0.5, 0.09375, ((0, 4), (1, 8)))
    return {"tokens": tokens, "weight": weight}


def reference(tokens, weight):
    gram = jnp.dot(weight, weight.T, preferred_element_type=jnp.float32)
    gram_b = gram.astype(jnp.bfloat16)
    orthonormal = (1.5 * weight.astype(jnp.float32) - 0.5 * jnp.dot(gram_b, weight, preferred_element_type=jnp.float32)).astype(jnp.bfloat16)
    return jnp.dot(tokens, orthonormal.T, preferred_element_type=jnp.float32).astype(jnp.bfloat16)
```

```python
import functools

import jax
import jax.numpy as jnp
from jax import lax
from jax.experimental import pallas as pl
from jax.experimental.pallas import tpu as pltpu
from jax.sharding import PartitionSpec as P

BF = jnp.bfloat16
F32 = jnp.float32
ANY = pl.BlockSpec(memory_space=pl.ANY)
SMEM = pl.BlockSpec(memory_space=pltpu.SMEM)
VMEM = pl.BlockSpec(memory_space=pltpu.VMEM)


def contract_last(left, right):
    return lax.dot_general(left, right, (((1,), (1,)), ((), ())), preferred_element_type=F32)


def contract(left, right):
    return lax.dot_general(left, right, (((1,), (0,)), ((), ())), preferred_element_type=F32)


def gathered_form(tokens, weight):
    rows = lax.all_gather(weight, "dp", axis=1, tiled=True)
    toks = lax.all_gather(tokens, "tensor", axis=0, tiled=True)
    first = contract_last(toks, rows)
    part = contract(first.astype(BF), rows).astype(BF)
    second = lax.psum(part, "tensor")
    return (1.5 * first - 0.5 * contract_last(second, rows)).astype(BF)


def call(body, ins, outs, scratch, flops):
    nbytes = sum(v.size * v.dtype.itemsize for v in ins) + sum(
        v.size * v.dtype.itemsize for v in outs
    )
    return pl.pallas_call(
        body,
        out_shape=outs,
        in_specs=[SMEM] + [ANY] * (len(ins) - 1),
        out_specs=[VMEM] * len(outs),
        scratch_shapes=scratch,
        compiler_params=pltpu.CompilerParams(vmem_limit_bytes=48 << 20),
        cost_estimate=pl.CostEstimate(flops=flops, bytes_accessed=nbytes, transcendentals=0),
    )(*ins)


def shape(dims, dtype):
    return jax.ShapeDtypeStruct(dims, dtype)


def tiles(extent, step=256):
    return [(at, min(step, extent - at)) for at in range(0, extent, step)]


def project(where, toks, parts, acc, width, rows, last):
    count = toks.shape[0]
    depth = width * len(parts)
    flat = [piece for _, pieces in parts for piece in pieces]

    def body(where_ref, t_ref, *refs):
        pieces = refs[: len(flat)]
        refs = refs[len(flat) :]
        if acc is not None:
            acc_ref, refs = refs[0], refs[1:]
        outs, (t_buf, w_buf, sem) = refs[: 2 if last else 1], refs[2 if last else 1 :]
        copies = []
        at = 0
        for k, (slot, own) in enumerate(parts):
            cols = pl.ds(k * width, width)
            src = pl.multiple_of(where_ref[slot] * width, width)
            copies.append((t_ref.at[:, pl.ds(src, width)], t_buf.at[:, cols]))
            row = 0
            for piece in own:
                height = piece.shape[0]
                copies.append((pieces[at], w_buf.at[pl.ds(row, height), cols]))
                row += height
                at += 1
        if acc is not None:
            copies.append((acc_ref, outs[0]))
        copies = [pltpu.make_async_copy(a, b, sem.at[i]) for i, (a, b) in enumerate(copies)]
        for c in copies:
            c.start()
        for c in copies:
            c.wait()
        for at, size in tiles(rows):
            term = contract_last(t_buf[...], w_buf[at : at + size, :])
            if acc is not None:
                term += outs[0][:, at : at + size]
            outs[0][:, at : at + size] = term
            if last:
                outs[1][:, at : at + size] = term.astype(BF)

    outs = [shape((count, rows), F32)] + ([shape((count, rows), BF)] if last else [])
    ins = [where, toks] + flat + ([acc] if acc is not None else [])
    scratch = [
        pltpu.VMEM((count, depth), BF),
        pltpu.VMEM((rows, depth), BF),
        pltpu.SemaphoreType.DMA((len(parts) + len(flat) + 1,)),
    ]
    return call(body, ins, outs, scratch, 2 * count * rows * depth)


def spread(where, p, chunks, width, rows, keep):
    count = p.shape[0]
    half = width // 2
    flat = [piece for pieces in chunks for piece in pieces]
    dtype = F32 if keep else BF

    def body(where_ref, p_ref, *refs):
        pieces, (out, p_buf, w_buf, sem) = refs[: len(flat)], refs[len(flat) :]
        core = where_ref[where.shape[0] - 1]
        src = pl.multiple_of((core if keep else 1 - core) * half, half)
        copies = [(p_ref, p_buf)]
        at = 0
        for k, own in enumerate(chunks):
            row = 0
            for piece in own:
                height = piece.shape[0]
                copies.append(
                    (pieces[at].at[:, pl.ds(src, half)], w_buf.at[k, pl.ds(row, height), :])
                )
                row += height
                at += 1
        copies = [pltpu.make_async_copy(a, b, sem.at[i]) for i, (a, b) in enumerate(copies)]
        for c in copies:
            c.start()
        for c in copies:
            c.wait()
        for k in range(len(chunks)):
            out[:, k * half : (k + 1) * half] = contract(p_buf[...], w_buf[k]).astype(dtype)

    scratch = [
        pltpu.VMEM((count, rows), BF),
        pltpu.VMEM((len(chunks), rows, half), BF),
        pltpu.SemaphoreType.DMA((1 + len(flat),)),
    ]
    flops = 2 * count * rows * half * len(chunks)
    return call(
        body, [where, p] + flat, [shape((count, half * len(chunks)), dtype)], scratch, flops
    )[0]


def collect(where, mine, theirs, chunks, acc, p, width, rows):
    count = mine.shape[0]
    half = width // 2
    flat = [piece for pieces in chunks for piece in pieces]
    extra = [v for v in (acc, p) if v is not None]

    def body(where_ref, mine_ref, theirs_ref, *refs):
        pieces, refs = refs[: len(flat)], refs[len(flat) :]
        more, (out, q_buf, w_buf, more_buf, sem) = refs[: len(extra)], refs[len(extra) :]
        core = where_ref[where.shape[0] - 1]
        copies = []
        at = 0
        for k, own in enumerate(chunks):
            for ref, side in ((mine_ref, core), (theirs_ref, 1 - core)):
                dst = pl.multiple_of(k * width + side * half, half)
                copies.append((ref.at[:, pl.ds(k * half, half)], q_buf.at[:, pl.ds(dst, half)]))
            row = 0
            for piece in own:
                height = piece.shape[0]
                copies.append(
                    (pieces[at], w_buf.at[pl.ds(row, height), pl.ds(k * width, width)])
                )
                row += height
                at += 1
        for i, ref in enumerate(more):
            copies.append((ref, more_buf.at[i]))
        copies = [pltpu.make_async_copy(a, b, sem.at[i]) for i, (a, b) in enumerate(copies)]
        for c in copies:
            c.start()
        for c in copies:
            c.wait()
        for at, size in tiles(rows):
            cols = slice(at, at + size)
            term = contract_last(q_buf[...], w_buf[cols, :])
            if acc is not None:
                term += more_buf[0, :, cols]
            if p is not None:
                term = 1.5 * more_buf[len(extra) - 1, :, cols] - 0.5 * term
            out[:, cols] = term.astype(out.dtype)

    depth = width * len(chunks)
    scratch = [
        pltpu.VMEM((count, depth), BF),
        pltpu.VMEM((rows, depth), BF),
        pltpu.VMEM((max(1, len(extra)), count, rows), F32),
        pltpu.SemaphoreType.DMA((2 * len(chunks) + len(flat) + len(extra),)),
    ]
    out = shape((count, rows), F32 if p is None else BF)
    ins = [where, mine, theirs] + flat + extra
    return call(body, ins, [out], scratch, 2 * count * rows * depth)[0]


def ring_form(n, tokens, weight):
    rows, width = weight.shape
    t = lax.axis_index("tensor")
    i = lax.axis_index("dp")
    steps = n // 2 - 1
    offsets = [0] + [o for s in range(1, steps + 1) for o in (-s, s)] + [steps + 1]
    ring = list(range(0, n, 2)) + list(range(n - 1, 0, -2))
    place = jnp.where(i % 2 == 0, i // 2, n - 1 - i // 2)
    spots = (place + jnp.array(offsets, jnp.int32) + n) % n
    source = jnp.where(spots < n // 2, 2 * spots, 2 * (n - 1 - spots) + 1)
    where = jnp.concatenate([source, (t % 2)[None]]).astype(jnp.int32)

    def up(v):
        return lax.ppermute(v, "dp", [(ring[i], ring[(i + 1) % n]) for i in range(n)])

    def down(v):
        return lax.ppermute(v, "dp", [(ring[(i + 1) % n], ring[i]) for i in range(n)])

    def over_x(v):
        return lax.ppermute(v, "tensor", [(t, t ^ 2) for t in range(4)])

    def over_core(v):
        return lax.ppermute(v, "tensor", [(t, t ^ 1) for t in range(4)])

    def gather(block):
        found = {0: [block]}
        u = d = block
        for s in range(1, steps + 1):
            u, d = up(u), down(d)
            found[-s], found[s] = [u], [d]
        half = block.shape[0] // 2
        found[steps + 1] = [up(u[:half]), down(d[half:])]
        return [found[o] for o in offsets]

    chunks = gather(weight)
    far = over_x(tokens)
    pair = jnp.where(t < 2, jnp.stack([tokens, far]), jnp.stack([far, tokens]))
    other = over_core(pair)
    quad = jnp.where(t % 2 == 0, jnp.stack([pair, other], 1), jnp.stack([other, pair], 1))
    toks = quad.reshape(4 * tokens.shape[0], tokens.shape[1])

    near = n - 3
    parts = list(enumerate(chunks))
    acc = project(where, toks, parts[:near], None, width, rows, False)[0]
    p, p_b = project(where, toks, parts[near:], acc, width, rows, True)

    groups = [chunks[0:2], chunks[2:4], chunks[4:6], chunks[6:8]]
    sums = []
    for bundle in (groups[:1], groups[1:]):
        joined = [c for g in bundle for c in g]
        give = over_core(spread(where, p_b, joined, width, rows, False))
        keep = spread(where, p_b, joined, width, rows, True)
        chip = keep + give.astype(F32)
        for k in range(len(bundle)):
            mine = chip[:, k * width : (k + 1) * width]
            sums.append((mine, over_x(mine.astype(BF))))
    out = None
    for g, (chip, far) in enumerate(sums):
        whole = (chip + far.astype(F32)).astype(BF)
        final = p if g == len(sums) - 1 else None
        out = collect(where, whole, over_core(whole), groups[g], out, final, width, rows)
    return out


def solution(mesh):
    n = mesh.shape["dp"]

    def on_device(tokens, weight):
        if mesh.shape["tensor"] == 4 and n == 8:
            return ring_form(n, tokens, weight)
        return gathered_form(tokens, weight)

    placed = (P(("dp", "tensor"), None), P("tensor", "dp"))
    return jax.shard_map(
        on_device, mesh=mesh, in_specs=placed, out_specs=P("dp", "tensor"), check_vma=False
    )
```

```python
import jax
import jax.numpy as jnp
from jax import lax
from jax.experimental import pallas as pl
from jax.experimental.pallas import tpu as pltpu
from jax.sharding import PartitionSpec as P

BF = jnp.bfloat16
F32 = jnp.float32
ANY = pl.BlockSpec(memory_space=pl.ANY)
HBM = pl.BlockSpec(memory_space=pltpu.HBM)
SMEM = pl.BlockSpec(memory_space=pltpu.SMEM)
VMEM = pl.BlockSpec(memory_space=pltpu.VMEM)
LATE = 256


def contract_last(left, right):
    return lax.dot_general(left, right, (((1,), (1,)), ((), ())), preferred_element_type=F32)


def contract(left, right):
    return lax.dot_general(left, right, (((1,), (0,)), ((), ())), preferred_element_type=F32)


def gathered_form(tokens, weight):
    rows = lax.all_gather(weight, "dp", axis=1, tiled=True)
    toks = lax.all_gather(tokens, "tensor", axis=0, tiled=True)
    first = contract_last(toks, rows)
    part = contract(first.astype(BF), rows).astype(BF)
    second = lax.psum(part, "tensor")
    return (1.5 * first - 0.5 * contract_last(second, rows)).astype(BF)


def tiles(extent, step=256):
    return [slice(at, min(at + step, extent)) for at in range(0, extent, step)]


def call(body, where, ins, outs, flops, after=(), leave=False, scratch=()):
    flat, tree = jax.tree.flatten(ins)
    after = list(after)
    n_in, n_out = len(flat), len(outs)

    scalars = [] if where is None else [where]

    def kernel(*refs):
        where_ref, refs = (refs[0], refs[1:]) if scalars else (None, refs)
        given = jax.tree.unflatten(tree, refs[:n_in])
        rest = refs[n_in + len(after) :]
        body(where_ref, given, rest[:n_out], *rest[n_out:])

    nbytes = sum(v.size * v.dtype.itemsize for v in flat)
    place = pltpu.HBM if leave else pltpu.VMEM
    flat = [pltpu.with_memory_space_constraint(v, place) for v in flat]
    return pl.pallas_call(
        kernel,
        out_shape=[pltpu.VMEM(*o) if isinstance(o, tuple) else o for o in outs],
        in_specs=[SMEM] * len(scalars) + [HBM if leave else VMEM] * n_in + [ANY] * len(after),
        out_specs=[VMEM] * n_out,
        scratch_shapes=[pltpu.SemaphoreType.DMA((n_out,))] if leave else list(scratch),
        compiler_params=pltpu.CompilerParams(vmem_limit_bytes=16 << 20),
        cost_estimate=pl.CostEstimate(flops=flops, bytes_accessed=nbytes, transcendentals=0),
    )(*scalars, *flat, *after)


def bounds(pieces):
    ends = [0]
    for piece in pieces:
        ends.append(ends[-1] + piece.shape[0])
    return ends


def cuts(chunks):
    edges = sorted({e for pieces in chunks for e in bounds(pieces)})
    return [
        slice(a + t.start, a + t.stop) for a, b in zip(edges, edges[1:]) for t in tiles(b - a)
    ]


def at_rows(pieces, rows, cols=slice(None)):
    for ref, start in zip(pieces, bounds(pieces)):
        if start <= rows.start and rows.stop <= start + ref.shape[0]:
            return ref[rows.start - start : rows.stop - start, cols]


def add_dots(pairs, acc=None):
    for left, right in pairs:
        term = contract_last(left, right)
        acc = term if acc is None else acc + term
    return acc


def ring_form(n, tokens, weight):
    rows, width = weight.shape
    own = tokens.shape[0]
    count = 4 * own
    half = width // 2
    early = rows - LATE
    middle = early // 2
    steps = n // 2 - 1
    wide = 4 * LATE
    square = (count, width)
    t = lax.axis_index("tensor")
    i = lax.axis_index("dp")
    offsets = [0] + [o for s in range(1, steps + 1) for o in (-s, s)] + [steps + 1]
    ring = list(range(0, n, 2)) + list(range(n - 1, 0, -2))
    place = jnp.where(i % 2 == 0, i // 2, n - 1 - i // 2)
    spots = (place + jnp.array(offsets, jnp.int32) + n) % n
    source = jnp.where(spots < n // 2, 2 * spots, 2 * (n - 1 - spots) + 1)
    core = t % 2
    x = t // 2
    slots = jnp.stack([t, 2 * (1 - x) + core, 2 * x + 1 - core, 2 * (1 - x) + 1 - core])
    where = jnp.concatenate([source, core[None], slots]).astype(jnp.int32)

    def up(v):
        return lax.ppermute(v, "dp", [(ring[i], ring[(i + 1) % n]) for i in range(n)])

    def down(v):
        return lax.ppermute(v, "dp", [(ring[(i + 1) % n], ring[i]) for i in range(n)])

    def over_x(v):
        return lax.ppermute(v, "tensor", [(t, t ^ 2) for t in range(4)])

    def over_core(v):
        return lax.ppermute(v, "tensor", [(t, t ^ 1) for t in range(4)])

    def copy_from(row):
        def body(where_ref, given, outs, sem):
            src = given[0].at[pl.ds(row, outs[0].shape[0]), :]
            copy = pltpu.make_async_copy(src, outs[0], sem.at[0])
            copy.start()
            copy.wait()

        return body

    def relay(where_ref, given, outs):
        for ref, out in zip(given, outs):
            out[...] = ref[...]

    def relayed(arrays, after):
        return call(relay, None, arrays, [(a.shape, a.dtype) for a in arrays], 0, after)

    def split(where_ref, given, outs):
        cut = outs[0].shape[0]
        outs[0][...] = given[0][:cut, :]
        outs[1][...] = given[1][cut:, :]

    def ends(u, d, after):
        h = u.shape[0] // 2
        return call(split, None, [u, d], [((h, width), BF), ((u.shape[0] - h, width), BF)], 0, after)

    def columns(k):
        return slice(k * width, (k + 1) * width)

    def halves(where_ref, own_half):
        side = where_ref[n]
        return pl.ds(pl.multiple_of((side if own_half else 1 - side) * half, half), half)

    def p_terms(tok, ks, chunks, acc_ref, put):
        for cut in cuts(chunks):
            pairs = [(tok[:, columns(k)], at_rows(c, cut)) for k, c in zip(ks, chunks)]
            put(cut, add_dots(pairs, None if acc_ref is None else acc_ref[:, cut]))

    def project(ks, acc, after=()):
        def body(where_ref, given, outs):
            tok, chunks, acc_ref = given

            def put(cols, value):
                outs[0][:, cols] = value

            p_terms(tok, ks, chunks, acc_ref, put)

        outs = [((count, early), F32)]
        flops = 2 * count * early * width * len(ks)
        return call(body, where, (toks, [w[k] for k in ks], acc), outs, flops, after)[0]

    far = over_x(tokens)
    first = call(copy_from(0), None, [weight], [((early, width), BF)], 0, (), True)[0]
    u1, d1 = up(first), down(first)
    late = call(copy_from(early), None, [weight], [((LATE, width), BF)], 0, [u1, d1], True)[0]
    u2, d2 = up(u1), down(d1)
    u3, d3 = up(u2), down(d2)
    w = [[first], [u1], [d1], [u2], [d2], [u3], [d3]]

    def arrange(where_ref, given, outs):
        for j, ref in enumerate(given):
            row = pl.multiple_of(where_ref[n + 1 + j] * own, own)
            for k in range(n):
                src = pl.multiple_of(where_ref[k] * width, width)
                outs[0][pl.ds(row, own), columns(k)] = ref[:, pl.ds(src, width)]

    toks = call(
        arrange,
        where,
        [tokens, far, over_core(tokens), over_core(far)],
        [((count, n * width), BF)],
        0,
    )[0]
    acc = project(list(range(n - 3)), None)
    late_far = over_x(late)
    a, b = ends(u3, d3, [acc, late_far])
    w.append([up(a), down(b)])
    acc = project([n - 3, n - 2], acc)

    def q_terms(p_ref, chunk, cols):
        total = None
        for ref, start in zip(chunk, bounds(chunk)):
            term = contract(p_ref[:, start : start + ref.shape[0]], ref[:, cols])
            total = term if total is None else total + term
        return total

    groups = [[0, 1], [2, 3], [4, 5], [6, 7]]
    near, more = groups[0] + groups[1], groups[2] + groups[3]
    unit = 2 * count * early * half
    wing = (count, half * len(near))

    def put_q(p_ref, chunks, cols, out):
        for at, chunk in enumerate(chunks):
            q = q_terms(p_ref, chunk, cols)
            out[:, at * half : (at + 1) * half] = q.astype(out.dtype)

    def first_give(where_ref, given, outs):
        tok, last, acc_ref, chunks = given

        def put(cols, value):
            outs[0][:, cols] = value
            outs[1][:, cols] = value.astype(BF)

        p_terms(tok, [n - 1], [last], acc_ref, put)
        put_q(outs[1], chunks, halves(where_ref, False), outs[2])

    p, p_b, give = call(
        first_give,
        where,
        (toks, w[-1], acc, [w[k] for k in near]),
        [((count, early), F32), ((count, early), BF), (wing, BF)],
        6 * unit,
    )

    def q_half(ks, own_half, dtype, after=()):
        def body(where_ref, given, outs):
            put_q(given[0], given[1], halves(where_ref, own_half), outs[0])

        ins = (p_b, [w[k] for k in ks])
        return call(body, where, ins, [(wing, dtype)], unit * len(ks), after)[0]

    def add_two(where_ref, given, outs):
        for g in range(2):
            q = given[0][:, columns(g)] + given[1][:, columns(g)].astype(F32)
            outs[g][...] = q
            outs[2 + g][...] = q.astype(BF)

    def q_pair(keep, got):
        return call(add_two, None, (keep, got), [(square, F32)] * 2 + [(square, BF)] * 2, 0)

    q0, q1, q0_b, q1_b = q_pair(q_half(near, True, F32), over_core(give))
    keep = q_half(more, True, F32, [q0_b])
    give = q_half(more, False, BF, [keep])
    q2, q3, q2_b, q3_b = q_pair(keep, over_core(give))

    def late_part(ks, accs, final, after=()):
        def body(where_ref, given, outs, *scratch):
            tok, lates, earlies, acc_refs = given
            p_out, g_out = scratch if final else outs

            def old(which, rows, cols):
                return None if accs is None else acc_refs[which][rows, cols]

            flat = [[m[0], m[1], o[0], o[1]] if len(m) == 2 else [m[0], o[0]] for m, o in lates]
            sets = [slice(j * LATE, (j + 1) * LATE) for j in range(4)]
            for cols in sets:
                pairs = [(tok[:, columns(k)], at_rows(f, cols)) for k, f in zip(ks, flat)]
                value = add_dots(pairs, old(0, slice(None), cols))
                p_out[:, cols] = value.astype(p_out.dtype)
                if final and cols.start == 0:
                    outs[0][...] = value
            for here in sets:
                for cols in cuts(earlies):
                    pairs = [(at_rows(f, here), at_rows(e, cols)) for f, e in zip(flat, earlies)]
                    g_out[here, cols] = add_dots(pairs, old(1, here, cols)).astype(g_out.dtype)
                cols = slice(early, rows)
                pairs = [(at_rows(f, here), at_rows(f, sets[0])) for f in flat]
                g_out[here, cols] = add_dots(pairs, old(1, here, cols)).astype(g_out.dtype)
            if final:
                for cols in tiles(rows):
                    outs[1][:, cols] = contract(p_out[...], g_out[:, cols])

        if final:
            outs = [((count, LATE), F32), ((count, rows), F32)]
            scratch = [pltpu.VMEM((count, wide), BF), pltpu.VMEM((wide, rows), BF)]
        else:
            outs = [((count, wide), F32), ((wide, rows), F32)]
            scratch = []
        flops = 2 * wide * (count + rows) * width * len(ks)
        ins = (toks, [v[k] for k in ks], [w[k] for k in ks], accs)
        return call(body, where, ins, outs, flops, after, False, scratch)

    def collect(ks, sides, out, final, after=()):
        def body(where_ref, given, outs):
            side_refs, chunks, out_ref, more = given
            for cols in cuts([e for e, _ in chunks]) + [slice(early, rows)]:
                term = None if out is None else out_ref[:, cols]
                for k, (early_rows, late_rows) in enumerate(chunks):
                    for ref, mine in zip(side_refs, (True, False)):
                        left = ref[:, k * half : (k + 1) * half]
                        if cols.start < early:
                            right = at_rows(early_rows, cols, halves(where_ref, mine))
                        else:
                            right = late_rows[0][0][:LATE, halves(where_ref, mine)]
                        term = add_dots([(left, right)], term)
                if final:
                    p_ref, late_ref, add_ref = more
                    p_val = p_ref[:, cols] if cols.start < early else late_ref[...]
                    term = 1.5 * p_val - 0.5 * (term + add_ref[:, cols])
                outs[0][:, cols] = term.astype(outs[0].dtype)

        outs = [jax.ShapeDtypeStruct((count, rows), BF) if final else ((count, rows), F32)]
        ins = (sides, [(w[k], v[k]) for k in ks], out, [p, p_late, out_late] if final else None)
        return call(body, where, ins, outs, 4 * count * rows * width, after)[0]

    def join(where_ref, given, outs):
        outs[0][:LATE, :] = given[0][...]
        outs[0][LATE:, :] = given[1][...]

    def turn(where_ref, given, outs):
        q_ref, far_ref, ring_refs, next_ref = given
        outs[0][...] = (q_ref[...] + far_ref[...].astype(F32)).astype(BF)
        if next_ref is not None:
            outs[1][...] = next_ref[...]
            relay(None, ring_refs, outs[2:4])
            if len(outs) > 4:
                split(None, ring_refs, outs[4:])

    def turned(q, far, ring_pair, next_q, last, after):
        outs = [(square, BF)]
        if next_q is not None:
            outs += [(square, BF)] + [((tall, width), BF)] * 2
            if last:
                outs += [((LATE, width), BF)] * 2
        return call(turn, None, (q, far, ring_pair, next_q), outs, 0, after)

    def both(pieces):
        return (pieces, [over_core(c) for c in pieces])

    tall = 2 * LATE
    block = call(join, None, [late, late_far], [((tall, width), BF)], 0, [p_b])[0]
    v = [both([block])]
    far, u, d = over_x(q0_b), up(block), down(block)
    sums = late_part([0], None, False, [q0_b])
    s0, nq, ru, rd = turned(q0, far, [u, d], q1_b, False, [sums[0], give])
    v += [both([ru]), both([rd])]
    far, u, d = over_x(nq), up(ru), down(rd)
    sums = late_part([1, 2], sums, False, [s0])
    s1, nq, ru, rd = turned(q1, far, [u, d], q2_b, False, [sums[0]])
    v += [both([ru]), both([rd])]
    far, u, d = over_x(nq), up(ru), down(rd)
    sums = late_part([3, 4], sums, False, [s1])
    out = collect(groups[0], [s0, over_core(s0)], None, False, [sums[0]])
    s2, nq, ru, rd, ra, rb = turned(q2, far, [u, d], q3_b, True, [out])
    v += [both([ru]), both([rd])]
    far, a, b = over_x(nq), up(ra), down(rb)
    sums = late_part([5, 6], sums, False, [s2])
    v += [both([a, b])]
    out = collect(groups[1], [s1, over_core(s1)], out, False, [sums[0]])
    out = collect(groups[2], [s2, over_core(s2)], out, False)
    s3 = turned(q3, far, None, None, False, [out])[0]
    p_late, out_late = late_part([n - 1], sums, True, [s3])
    return collect(groups[3], [s3, over_core(s3)], out, True)


def solution(mesh):
    n = mesh.shape["dp"]

    def on_device(tokens, weight):
        if mesh.shape["tensor"] == 4 and n == 8:
            return ring_form(n, tokens, weight)
        return gathered_form(tokens, weight)

    placed = (P(("dp", "tensor"), None), P("tensor", "dp"))
    return jax.shard_map(
        on_device, mesh=mesh, in_specs=placed, out_specs=P("dp", "tensor"), check_vma=False
    )
```

```python
import jax
import jax.numpy as jnp
from jax import lax
from jax.experimental import pallas as pl
from jax.experimental.pallas import tpu as pltpu
from jax.sharding import PartitionSpec as P

BF = jnp.bfloat16
F32 = jnp.float32
ANY = pl.BlockSpec(memory_space=pl.ANY)
HBM = pl.BlockSpec(memory_space=pltpu.HBM)
VMEM = pl.BlockSpec(memory_space=pltpu.VMEM)
LATE = 256


def contract_last(left, right):
    return lax.dot_general(left, right, (((1,), (1,)), ((), ())), preferred_element_type=F32)


def contract(left, right):
    return lax.dot_general(left, right, (((1,), (0,)), ((), ())), preferred_element_type=F32)


def gathered_form(tokens, weight):
    rows = lax.all_gather(weight, "dp", axis=1, tiled=True)
    toks = lax.all_gather(tokens, "tensor", axis=0, tiled=True)
    first = contract_last(toks, rows)
    part = contract(first.astype(BF), rows).astype(BF)
    second = lax.psum(part, "tensor")
    return (1.5 * first - 0.5 * contract_last(second, rows)).astype(BF)


def tiles(extent, step=256):
    return [slice(at, min(at + step, extent)) for at in range(0, extent, step)]


def call(body, ins, outs, flops, after=(), leave=False, scratch=()):
    flat, tree = jax.tree.flatten(ins)
    after = list(after)
    n_in, n_out = len(flat), len(outs)

    def kernel(*refs):
        given = jax.tree.unflatten(tree, refs[:n_in])
        rest = refs[n_in + len(after) :]
        body(given, rest[:n_out], *rest[n_out:])

    nbytes = sum(v.size * v.dtype.itemsize for v in flat)
    place = pltpu.HBM if leave else pltpu.VMEM
    flat = [pltpu.with_memory_space_constraint(v, place) for v in flat]
    return pl.pallas_call(
        kernel,
        out_shape=[pltpu.VMEM(*o) if isinstance(o, tuple) else o for o in outs],
        in_specs=[HBM if leave else VMEM] * n_in + [ANY] * len(after),
        out_specs=[VMEM] * n_out,
        scratch_shapes=[pltpu.SemaphoreType.DMA((n_out,))] if leave else list(scratch),
        compiler_params=pltpu.CompilerParams(vmem_limit_bytes=16 << 20),
        cost_estimate=pl.CostEstimate(flops=flops // 20, bytes_accessed=nbytes // 20, transcendentals=0),
    )(*flat, *after)


def bounds(pieces):
    ends = [0]
    for piece in pieces:
        ends.append(ends[-1] + piece.shape[0])
    return ends


def cuts(chunks):
    edges = sorted({e for pieces in chunks for e in bounds(pieces)})
    return [
        slice(a + t.start, a + t.stop) for a, b in zip(edges, edges[1:]) for t in tiles(b - a)
    ]


def at_rows(pieces, rows, cols=slice(None)):
    for ref, start in zip(pieces, bounds(pieces)):
        if start <= rows.start and rows.stop <= start + ref.shape[0]:
            return ref[rows.start - start : rows.stop - start, cols]


def add_dots(pairs, acc=None):
    for left, right in pairs:
        term = contract_last(left, right)
        acc = term if acc is None else acc + term
    return acc


def ring_form(n, tokens, weight):
    rows, width = weight.shape
    own = tokens.shape[0]
    count = 4 * own
    half = width // 2
    early = rows - LATE
    middle = early // 2
    steps = n // 2 - 1
    wide = 4 * LATE
    square = (count, width)
    offsets = [0] + [o for s in range(1, steps + 1) for o in (-s, s)] + [steps + 1]
    ring = list(range(0, n, 2)) + list(range(n - 1, 0, -2))

    def source(k):
        i = lax.axis_index("dp")
        place = jnp.where(lax.rem(i, 2) == 0, i // 2, n - 1 - i // 2)
        spot = lax.rem(place + offsets[k] + n, n)
        return jnp.where(spot < n // 2, 2 * spot, 2 * (n - 1 - spot) + 1)

    def side(mine):
        core = lax.rem(lax.axis_index("tensor"), 2)
        return core if mine else 1 - core

    def up(v):
        return lax.ppermute(v, "dp", [(ring[i], ring[(i + 1) % n]) for i in range(n)])

    def down(v):
        return lax.ppermute(v, "dp", [(ring[(i + 1) % n], ring[i]) for i in range(n)])

    def over_x(v):
        return lax.ppermute(v, "tensor", [(t, t ^ 2) for t in range(4)])

    def over_core(v):
        return lax.ppermute(v, "tensor", [(t, t ^ 1) for t in range(4)])

    def copy_from(row):
        def body(given, outs, sem):
            src = given[0].at[pl.ds(row, outs[0].shape[0]), :]
            copy = pltpu.make_async_copy(src, outs[0], sem.at[0])
            copy.start()
            copy.wait()

        return body

    def relay(given, outs):
        for ref, out in zip(given, outs):
            out[...] = ref[...]

    def relayed(arrays, after):
        return call(relay, arrays, [(a.shape, a.dtype) for a in arrays], 0, after)

    def split(given, outs):
        cut = outs[0].shape[0]
        outs[0][...] = given[0][:cut, :]
        outs[1][...] = given[1][cut:, :]

    def ends(u, d, after):
        h = u.shape[0] // 2
        return call(split, [u, d], [((h, width), BF), ((u.shape[0] - h, width), BF)], 0, after)

    def columns(k):
        return slice(k * width, (k + 1) * width)

    def halves(mine):
        return pl.ds(pl.multiple_of(side(mine) * half, half), half)

    def p_terms(tok, ks, chunks, acc_ref, put):
        for cut in cuts(chunks):
            pairs = [(tok[:, columns(k)], at_rows(c, cut)) for k, c in zip(ks, chunks)]
            put(cut, add_dots(pairs, None if acc_ref is None else acc_ref[:, cut]))

    def project(ks, acc, after=()):
        def body(given, outs):
            tok, chunks, acc_ref = given

            def put(cols, value):
                outs[0][:, cols] = value

            p_terms(tok, ks, chunks, acc_ref, put)

        outs = [((count, early), F32)]
        flops = 2 * count * early * width * len(ks)
        return call(body, (toks, [w[k] for k in ks], acc), outs, flops, after)[0]

    far = over_x(tokens)
    first = call(copy_from(0), [weight], [((early, width), BF)], 0, (), True)[0]
    u1, d1 = up(first), down(first)
    late = call(copy_from(early), [weight], [((LATE, width), BF)], 0, [u1, d1], True)[0]
    u2, d2 = up(u1), down(d1)
    u3, d3 = up(u2), down(d2)
    w = [[first], [u1], [d1], [u2], [d2], [u3], [d3]]

    def arrange(given, outs):
        core, x = side(True), lax.axis_index("tensor") // 2
        slots = [2 * x + core, 2 * (1 - x) + core, 2 * x + 1 - core, 2 * (1 - x) + 1 - core]
        for ref, slot in zip(given, slots):
            row = pl.multiple_of(slot * own, own)
            for k in range(n):
                src = pl.multiple_of(source(k) * width, width)
                outs[0][pl.ds(row, own), columns(k)] = ref[:, pl.ds(src, width)]

    toks = call(
        arrange,
        [tokens, far, over_core(tokens), over_core(far)],
        [((count, n * width), BF)],
        0,
    )[0]
    acc = project(list(range(n - 3)), None)
    late_far = over_x(late)
    a, b = ends(u3, d3, [acc, late_far])
    w.append([up(a), down(b)])
    acc = project([n - 3, n - 2], acc)

    def q_terms(p_ref, chunk, cols):
        total = None
        for ref, start in zip(chunk, bounds(chunk)):
            term = contract(p_ref[:, start : start + ref.shape[0]], ref[:, cols])
            total = term if total is None else total + term
        return total

    sizes = [5 * half // 2, 5 * half // 2, 2 * half, half]
    starts = [sum(sizes[:g]) for g in range(len(sizes))]

    def spots(g):
        found = []
        for k in range(n):
            lo = max(starts[g], k * half)
            hi = min(starts[g] + sizes[g], (k + 1) * half)
            if lo < hi:
                found.append((k, slice(lo - starts[g], hi - starts[g]), lo - k * half, hi - lo))
        return found

    def block_columns(mine, offset, size):
        return pl.ds(pl.multiple_of(side(mine) * half + offset, 128), size)

    def put_q(p_ref, g, chunks, mine, out):
        for (_, here, offset, size), chunk in zip(spots(g), chunks):
            q = q_terms(p_ref, chunk, block_columns(mine, offset, size))
            out[:, here] = q.astype(out.dtype)

    def part_of_w(g):
        return [w[k] for k, *_ in spots(g)]

    def first_give(given, outs):
        tok, last, acc_ref, chunks = given

        def put(cols, value):
            outs[0][:, cols] = value
            outs[1][:, cols] = value.astype(BF)

        p_terms(tok, [n - 1], [last], acc_ref, put)
        put_q(outs[1], 0, chunks, False, outs[2])

    def q_flops(g):
        return 2 * count * early * sizes[g]

    p, p_b, give = call(
        first_give,
        (toks, w[-1], acc, part_of_w(0)),
        [((count, early), F32), ((count, early), BF), ((count, sizes[0]), BF)],
        2 * q_flops(0),
    )

    def q_part(gs, mine, dtype, after=()):
        def body(given, outs):
            start = 0
            for at, (g, chunks) in enumerate(zip(gs, given[1])):
                out = outs[at] if mine else outs[0].at[:, start : start + sizes[g]]
                put_q(given[0], g, chunks, mine, out)
                start += sizes[g]

        outs = [((count, sizes[g]), dtype) for g in gs]
        if not mine:
            outs = [((count, sum(sizes[g] for g in gs)), dtype)]
        ins = (p_b, [part_of_w(g) for g in gs])
        return call(body, ins, outs, sum(q_flops(g) for g in gs), after)

    def add_two(given, outs):
        keep, got = given
        start = 0
        for at, a in enumerate(keep):
            q = a[...] + got[:, start : start + a.shape[1]].astype(F32)
            outs[2 * at][...] = q
            outs[2 * at + 1][...] = q.astype(BF)
            start += a.shape[1]

    def q_sum(keep, give):
        outs = [((count, k.shape[1]), dtype) for k in keep for dtype in (F32, BF)]
        return call(add_two, (keep, over_core(give)), outs, 0)

    keep = q_part([0], True, F32)
    give1 = q_part([1], False, BF, keep)[0]
    q0, q0_b = q_sum(keep, give)
    keep = q_part([1], True, F32, [q0_b])
    q1, q1_b = q_sum(keep, give1)
    keep = q_part([2, 3], True, F32, [q0_b])
    give = q_part([2, 3], False, BF, keep)[0]
    q2, q2_b, q3, q3_b = q_sum(keep, give)

    def late_part(ks, accs, final, after=(), more=None):
        def body(given, outs, *scratch):
            tok, lates, earlies, acc_refs, more = given
            p_out, g_out = scratch if final else outs

            def old(which, rows, cols):
                return None if accs is None else acc_refs[which][rows, cols]

            flat = [[m[0], m[1], o[0], o[1]] if len(m) == 2 else [m[0], o[0]] for m, o in lates]
            sets = [slice(j * LATE, (j + 1) * LATE) for j in range(4)]
            for cols in sets:
                pairs = [(tok[:, columns(k)], at_rows(f, cols)) for k, f in zip(ks, flat)]
                value = add_dots(pairs, old(0, slice(None), cols))
                p_out[:, cols] = value.astype(p_out.dtype)
                if final and cols.start == 0:
                    p_own = value
            for here in sets:
                for cols in cuts(earlies):
                    pairs = [(at_rows(f, here), at_rows(e, cols)) for f, e in zip(flat, earlies)]
                    g_out[here, cols] = add_dots(pairs, old(1, here, cols)).astype(g_out.dtype)
                cols = slice(early, rows)
                pairs = [(at_rows(f, here), at_rows(f, sets[0])) for f in flat]
                g_out[here, cols] = add_dots(pairs, old(1, here, cols)).astype(g_out.dtype)
            if final:
                p_ref, q_ref = more
                for cols in tiles(early) + [slice(early, rows)]:
                    p_val = p_ref[:, cols] if cols.start < early else p_own
                    term = q_ref[:, cols] + contract(p_out[...], g_out[:, cols])
                    outs[0][:, cols] = 1.5 * p_val - 0.5 * term

        if final:
            outs = [((count, rows), F32)]
            scratch = [pltpu.VMEM((count, wide), BF), pltpu.VMEM((wide, rows), BF)]
        else:
            outs = [((count, wide), F32), ((wide, rows), F32)]
            scratch = []
        flops = 2 * wide * (count + rows) * width * len(ks)
        ins = (toks, [v[k] for k in ks], [w[k] for k in ks], accs, more)
        return call(body, ins, outs, flops, after, False, scratch)

    def collect(g, sides, out, final, after=()):
        def body(given, outs):
            side_refs, chunks, base_ref = given
            for cols in cuts([e for e, _ in chunks]) + [slice(early, rows)]:
                term = None if out is None or final else base_ref[:, cols]
                for (_, here, offset, size), (early_rows, late_rows) in zip(spots(g), chunks):
                    for ref, mine in zip(side_refs, (True, False)):
                        left = ref[:, here]
                        block_cols = block_columns(mine, offset, size)
                        if cols.start < early:
                            right = at_rows(early_rows, cols, block_cols)
                        else:
                            right = late_rows[0][0][:LATE, block_cols]
                        term = add_dots([(left, right)], term)
                if final:
                    term = base_ref[:, cols] - 0.5 * term
                outs[0][:, cols] = term.astype(outs[0].dtype)

        outs = [jax.ShapeDtypeStruct((count, rows), BF) if final else ((count, rows), F32)]
        ins = (sides, [(w[k], v[k]) for k, *_ in spots(g)], out)
        return call(body, ins, outs, 4 * count * rows * sizes[g], after)[0]

    def join(given, outs):
        outs[0][:LATE, :] = given[0][...]
        outs[0][LATE:, :] = given[1][...]

    def turn(given, outs):
        q_ref, far_ref, next_ref = given
        outs[0][...] = (q_ref[...] + far_ref[...].astype(F32)).astype(BF)
        if next_ref is not None:
            outs[1][...] = next_ref[...]

    def turned(q, far, next_q, after):
        outs = [(q.shape, BF)] + ([] if next_q is None else [(next_q.shape, BF)])
        return call(turn, (q, far, next_q), outs, 0, after)

    def step(given, outs):
        relay(given, outs[:2])
        if len(outs) > 2:
            split(given, outs[2:])

    def stepped(u, d, last, after):
        outs = [(u.shape, BF), (d.shape, BF)] + ([((LATE, width), BF)] * 2 if last else [])
        return call(step, [u, d], outs, 0, after)

    def both(pieces):
        return (pieces, [over_core(c) for c in pieces])

    tall = 2 * LATE
    block = call(join, [late, late_far], [((tall, width), BF)], 0, [p_b])[0]
    v = [both([block])]
    u, d = up(block), down(block)
    far = over_x(q0_b)
    sums = late_part([0], None, False, [q0_b])
    ru, rd = stepped(u, d, False, [sums[0]])
    v += [both([ru]), both([rd])]
    u, d = up(ru), down(rd)
    s0, nq = turned(q0, far, q1_b, [ru, q2_b])
    far = over_x(nq)
    sums = late_part([1, 2], sums, False, [s0])
    ru, rd = stepped(u, d, False, [sums[0]])
    v += [both([ru]), both([rd])]
    u, d = up(ru), down(rd)
    out = collect(0, [s0, over_core(s0)], None, False, [ru])
    s1, nq = turned(q1, far, q2_b, [out])
    far = over_x(nq)
    sums = late_part([3, 4], sums, False, [s1])
    ru, rd, a, b = stepped(u, d, True, [sums[0]])
    v += [both([ru]), both([rd])]
    a, b = up(a), down(b)
    out = collect(1, [s1, over_core(s1)], out, False, [ru])
    a, b = stepped(a, b, False, [out])
    v += [both([a, b])]
    s2, nq = turned(q2, far, q3_b, [a])
    far = over_x(nq)
    sums = late_part([5, 6], sums, False, [s2])
    out = collect(2, [s2, over_core(s2)], out, False, sums[:1])
    out = late_part([n - 1], sums, True, [], [p, out])[0]
    s3 = turned(q3, far, None, [out])[0]
    return collect(3, [s3, over_core(s3)], out, True)


def solution(mesh):
    n = mesh.shape["dp"]

    def on_device(tokens, weight):
        if mesh.shape["tensor"] == 4 and n == 8:
            return ring_form(n, tokens, weight)
        return gathered_form(tokens, weight)

    placed = (P(("dp", "tensor"), None), P("tensor", "dp"))
    return jax.shard_map(
        on_device, mesh=mesh, in_specs=placed, out_specs=P("dp", "tensor"), check_vma=False
    )
```

```python
import jax
import jax.numpy as jnp
from jax import lax
from jax.experimental import pallas as pl
from jax.experimental.pallas import tpu as pltpu
from jax.sharding import PartitionSpec as P

BF = jnp.bfloat16
F32 = jnp.float32
ANY = pl.BlockSpec(memory_space=pl.ANY)
HBM = pl.BlockSpec(memory_space=pltpu.HBM)
VMEM = pl.BlockSpec(memory_space=pltpu.VMEM)
LATE = 256


def contract_last(left, right):
    return lax.dot_general(left, right, (((1,), (1,)), ((), ())), preferred_element_type=F32)


def contract(left, right):
    return lax.dot_general(left, right, (((1,), (0,)), ((), ())), preferred_element_type=F32)


def gathered_form(tokens, weight):
    rows = lax.all_gather(weight, "dp", axis=1, tiled=True)
    toks = lax.all_gather(tokens, "tensor", axis=0, tiled=True)
    first = contract_last(toks, rows)
    part = contract(first.astype(BF), rows).astype(BF)
    second = lax.psum(part, "tensor")
    return (1.5 * first - 0.5 * contract_last(second, rows)).astype(BF)


def tiles(extent, step=256):
    return [slice(at, min(at + step, extent)) for at in range(0, extent, step)]


def call(body, ins, outs, flops, after=(), leave=False, scratch=()):
    flat, tree = jax.tree.flatten(ins)
    after = list(after)
    n_in, n_out = len(flat), len(outs)

    def kernel(*refs):
        given = jax.tree.unflatten(tree, refs[:n_in])
        rest = refs[n_in + len(after) :]
        body(given, rest[:n_out], *rest[n_out:])

    nbytes = sum(v.size * v.dtype.itemsize for v in flat)
    place = pltpu.HBM if leave else pltpu.VMEM
    flat = [pltpu.with_memory_space_constraint(v, place) for v in flat]
    return pl.pallas_call(
        kernel,
        out_shape=[pltpu.VMEM(*o) if isinstance(o, tuple) else o for o in outs],
        in_specs=[HBM if leave else VMEM] * n_in + [ANY] * len(after),
        out_specs=[VMEM] * n_out,
        scratch_shapes=[pltpu.SemaphoreType.DMA((n_out,))] if leave else list(scratch),
        compiler_params=pltpu.CompilerParams(vmem_limit_bytes=16 << 20),
        cost_estimate=pl.CostEstimate(flops=flops // 20, bytes_accessed=nbytes // 20, transcendentals=0),
    )(*flat, *after)


def bounds(pieces):
    ends = [0]
    for piece in pieces:
        ends.append(ends[-1] + piece.shape[0])
    return ends


def cuts(chunks):
    edges = sorted({e for pieces in chunks for e in bounds(pieces)})
    return [
        slice(a + t.start, a + t.stop) for a, b in zip(edges, edges[1:]) for t in tiles(b - a)
    ]


def at_rows(pieces, rows, cols=slice(None)):
    for ref, start in zip(pieces, bounds(pieces)):
        if start <= rows.start and rows.stop <= start + ref.shape[0]:
            return ref[rows.start - start : rows.stop - start, cols]


def add_dots(pairs, acc=None):
    for left, right in pairs:
        term = contract_last(left, right)
        acc = term if acc is None else acc + term
    return acc


def ring_form(n, tokens, weight):
    rows, width = weight.shape
    own = tokens.shape[0]
    count = 4 * own
    half = width // 2
    early = rows - LATE
    middle = early // 2
    steps = n // 2 - 1
    wide = 4 * LATE
    square = (count, width)
    offsets = [0] + [o for s in range(1, steps + 1) for o in (-s, s)] + [steps + 1]
    ring = list(range(0, n, 2)) + list(range(n - 1, 0, -2))

    def source(k):
        i = lax.axis_index("dp")
        place = jnp.where(lax.rem(i, 2) == 0, i // 2, n - 1 - i // 2)
        spot = lax.rem(place + offsets[k] + n, n)
        return jnp.where(spot < n // 2, 2 * spot, 2 * (n - 1 - spot) + 1)

    def side(mine):
        core = lax.rem(lax.axis_index("tensor"), 2)
        return core if mine else 1 - core

    def up(v):
        return lax.ppermute(v, "dp", [(ring[i], ring[(i + 1) % n]) for i in range(n)])

    def down(v):
        return lax.ppermute(v, "dp", [(ring[(i + 1) % n], ring[i]) for i in range(n)])

    def over_x(v):
        return lax.ppermute(v, "tensor", [(t, t ^ 2) for t in range(4)])

    def over_core(v):
        return lax.ppermute(v, "tensor", [(t, t ^ 1) for t in range(4)])

    def copy_from(row):
        def body(given, outs, sem):
            src = given[0].at[pl.ds(row, outs[0].shape[0]), :]
            copy = pltpu.make_async_copy(src, outs[0], sem.at[0])
            copy.start()
            copy.wait()

        return body

    def relay(given, outs):
        for ref, out in zip(given, outs):
            out[...] = ref[...]

    def relayed(arrays, after):
        return call(relay, arrays, [(a.shape, a.dtype) for a in arrays], 0, after)

    def split(given, outs):
        cut = outs[0].shape[0]
        outs[0][...] = given[0][:cut, :]
        outs[1][...] = given[1][cut:, :]

    def ends(u, d, after):
        h = u.shape[0] // 2
        return call(split, [u, d], [((h, width), BF), ((u.shape[0] - h, width), BF)], 0, after)

    def columns(k):
        return slice(k * width, (k + 1) * width)

    def halves(mine):
        return pl.ds(pl.multiple_of(side(mine) * half, half), half)

    def p_terms(tok, ks, chunks, acc_ref, put):
        for cut in cuts(chunks):
            pairs = [(tok[:, columns(k)], at_rows(c, cut)) for k, c in zip(ks, chunks)]
            put(cut, add_dots(pairs, None if acc_ref is None else acc_ref[:, cut]))

    def project(ks, acc, after=()):
        def body(given, outs):
            tok, chunks, acc_ref = given

            def put(cols, value):
                outs[0][:, cols] = value

            p_terms(tok, ks, chunks, acc_ref, put)

        outs = [((count, early), F32)]
        flops = 2 * count * early * width * len(ks)
        return call(body, (toks, [w[k] for k in ks], acc), outs, flops, after)[0]

    far = over_x(tokens)
    first = call(copy_from(0), [weight], [((early, width), BF)], 0, (), True)[0]
    u1, d1 = up(first), down(first)
    late = call(copy_from(early), [weight], [((LATE, width), BF)], 0, [u1, d1], True)[0]
    u2, d2 = up(u1), down(d1)
    u3, d3 = up(u2), down(d2)
    w = [[first], [u1], [d1], [u2], [d2], [u3], [d3]]

    def arrange(given, outs):
        core, x = side(True), lax.axis_index("tensor") // 2
        slots = [2 * x + core, 2 * (1 - x) + core, 2 * x + 1 - core, 2 * (1 - x) + 1 - core]
        for ref, slot in zip(given, slots):
            row = pl.multiple_of(slot * own, own)
            for k in range(n):
                src = pl.multiple_of(source(k) * width, width)
                outs[0][pl.ds(row, own), columns(k)] = ref[:, pl.ds(src, width)]

    toks = call(
        arrange,
        [tokens, far, over_core(tokens), over_core(far)],
        [((count, n * width), BF)],
        0,
    )[0]
    acc = project(list(range(n - 3)), None)
    late_far = over_x(late)
    a, b = ends(u3, d3, [acc, late_far])
    w.append([up(a), down(b)])
    acc = project([n - 3, n - 2], acc)

    def q_terms(p_ref, chunk, cols):
        total = None
        for ref, start in zip(chunk, bounds(chunk)):
            term = contract(p_ref[:, start : start + ref.shape[0]], ref[:, cols])
            total = term if total is None else total + term
        return total

    sizes = [u * half // 2 for u in (4,5,5,2)]
    starts = [sum(sizes[:g]) for g in range(len(sizes))]

    def spots(g):
        found = []
        for k in range(n):
            lo = max(starts[g], k * half)
            hi = min(starts[g] + sizes[g], (k + 1) * half)
            if lo < hi:
                found.append((k, slice(lo - starts[g], hi - starts[g]), lo - k * half, hi - lo))
        return found

    def block_columns(mine, offset, size):
        return pl.ds(pl.multiple_of(side(mine) * half + offset, 128), size)

    def put_q(p_ref, g, chunks, mine, out):
        for (_, here, offset, size), chunk in zip(spots(g), chunks):
            q = q_terms(p_ref, chunk, block_columns(mine, offset, size))
            out[:, here] = q.astype(out.dtype)

    def part_of_w(g):
        return [w[k] for k, *_ in spots(g)]

    def first_give(given, outs):
        tok, last, acc_ref, chunks = given

        def put(cols, value):
            outs[0][:, cols] = value
            outs[1][:, cols] = value.astype(BF)

        p_terms(tok, [n - 1], [last], acc_ref, put)
        put_q(outs[1], 0, chunks, False, outs[2])

    def q_flops(g):
        return 2 * count * early * sizes[g]

    p, p_b, give = call(
        first_give,
        (toks, w[-1], acc, part_of_w(0)),
        [((count, early), F32), ((count, early), BF), ((count, sizes[0]), BF)],
        2 * q_flops(0),
    )

    def q_part(gs, mine, dtype, after=()):
        def body(given, outs):
            start = 0
            for at, (g, chunks) in enumerate(zip(gs, given[1])):
                out = outs[at] if mine else outs[0].at[:, start : start + sizes[g]]
                put_q(given[0], g, chunks, mine, out)
                start += sizes[g]

        outs = [((count, sizes[g]), dtype) for g in gs]
        if not mine:
            outs = [((count, sum(sizes[g] for g in gs)), dtype)]
        ins = (p_b, [part_of_w(g) for g in gs])
        return call(body, ins, outs, sum(q_flops(g) for g in gs), after)

    def add_two(given, outs):
        keep, got = given
        start = 0
        for at, a in enumerate(keep):
            q = a[...] + got[:, start : start + a.shape[1]].astype(F32)
            outs[2 * at][...] = q
            outs[2 * at + 1][...] = q.astype(BF)
            start += a.shape[1]

    def q_sum(keep, give):
        outs = [((count, k.shape[1]), dtype) for k in keep for dtype in (F32, BF)]
        return call(add_two, (keep, over_core(give)), outs, 0)

    keep = q_part([0], True, F32)
    give1 = q_part([1], False, BF, keep)[0]
    q0, q0_b = q_sum(keep, give)
    keep = q_part([1], True, F32, [q0_b])
    q1, q1_b = q_sum(keep, give1)
    keep = q_part([2, 3], True, F32, [q0_b])
    give = q_part([2, 3], False, BF, keep)[0]
    q2, q2_b, q3, q3_b = q_sum(keep, give)

    def late_part(ks, accs, final, after=(), more=None):
        def body(given, outs, *scratch):
            tok, lates, earlies, acc_refs, more = given
            p_out, g_out = scratch if final else outs

            def old(which, rows, cols):
                return None if accs is None else acc_refs[which][rows, cols]

            flat = [[m[0], m[1], o[0], o[1]] if len(m) == 2 else [m[0], o[0]] for m, o in lates]
            sets = [slice(j * LATE, (j + 1) * LATE) for j in range(4)]
            for cols in sets:
                pairs = [(tok[:, columns(k)], at_rows(f, cols)) for k, f in zip(ks, flat)]
                value = add_dots(pairs, old(0, slice(None), cols))
                p_out[:, cols] = value.astype(p_out.dtype)
                if final and cols.start == 0:
                    p_own = value
            for here in sets:
                for cols in cuts(earlies):
                    pairs = [(at_rows(f, here), at_rows(e, cols)) for f, e in zip(flat, earlies)]
                    g_out[here, cols] = add_dots(pairs, old(1, here, cols)).astype(g_out.dtype)
                cols = slice(early, rows)
                pairs = [(at_rows(f, here), at_rows(f, sets[0])) for f in flat]
                g_out[here, cols] = add_dots(pairs, old(1, here, cols)).astype(g_out.dtype)
            if final:
                p_ref, q_ref = more
                for cols in tiles(early) + [slice(early, rows)]:
                    p_val = p_ref[:, cols] if cols.start < early else p_own
                    term = q_ref[:, cols] + contract(p_out[...], g_out[:, cols])
                    outs[0][:, cols] = 1.5 * p_val - 0.5 * term

        if final:
            outs = [((count, rows), F32)]
            scratch = [pltpu.VMEM((count, wide), BF), pltpu.VMEM((wide, rows), BF)]
        else:
            outs = [((count, wide), F32), ((wide, rows), F32)]
            scratch = []
        flops = 2 * wide * (count + rows) * width * len(ks)
        ins = (toks, [v[k] for k in ks], [w[k] for k in ks], accs, more)
        return call(body, ins, outs, flops, after, False, scratch)

    def collect(g, sides, out, final, after=()):
        def body(given, outs):
            side_refs, chunks, base_ref = given
            for cols in cuts([e for e, _ in chunks]) + [slice(early, rows)]:
                term = None if out is None or final else base_ref[:, cols]
                for (_, here, offset, size), (early_rows, late_rows) in zip(spots(g), chunks):
                    for ref, mine in zip(side_refs, (True, False)):
                        left = ref[:, here]
                        block_cols = block_columns(mine, offset, size)
                        if cols.start < early:
                            right = at_rows(early_rows, cols, block_cols)
                        else:
                            right = late_rows[0][0][:LATE, block_cols]
                        term = add_dots([(left, right)], term)
                if final:
                    term = base_ref[:, cols] - 0.5 * term
                outs[0][:, cols] = term.astype(outs[0].dtype)

        outs = [jax.ShapeDtypeStruct((count, rows), BF) if final else ((count, rows), F32)]
        ins = (sides, [(w[k], v[k]) for k, *_ in spots(g)], out)
        return call(body, ins, outs, 4 * count * rows * sizes[g], after)[0]

    def join(given, outs):
        outs[0][:LATE, :] = given[0][...]
        outs[0][LATE:, :] = given[1][...]

    def turn(given, outs):
        q_ref, far_ref, next_ref = given
        outs[0][...] = (q_ref[...] + far_ref[...].astype(F32)).astype(BF)
        if next_ref is not None:
            outs[1][...] = next_ref[...]

    def turned(q, far, next_q, after):
        outs = [(q.shape, BF)] + ([] if next_q is None else [(next_q.shape, BF)])
        return call(turn, (q, far, next_q), outs, 0, after)

    def step(given, outs):
        relay(given, outs[:2])
        if len(outs) > 2:
            split(given, outs[2:])

    def stepped(u, d, last, after):
        outs = [(u.shape, BF), (d.shape, BF)] + ([((LATE, width), BF)] * 2 if last else [])
        return call(step, [u, d], outs, 0, after)

    def both(pieces):
        return (pieces, [over_core(c) for c in pieces])

    tall = 2 * LATE
    block = call(join, [late, late_far], [((tall, width), BF)], 0, [p_b])[0]
    v = [both([block])]
    u, d = up(block), down(block)
    far = over_x(q0_b)
    sums = late_part([0], None, False, [q0_b])
    ru, rd = stepped(u, d, False, [sums[0], give])
    v += [both([ru]), both([rd])]
    u, d = up(ru), down(rd)
    s0, nq = turned(q0, far, q1_b, [ru, q2_b])
    far = over_x(nq)
    ru, rd = stepped(u, d, False, [s0])
    v += [both([ru]), both([rd])]
    u, d = up(ru), down(rd)
    sums = late_part([1, 2], sums, False, [ru])
    out = collect(0, [s0, over_core(s0)], None, False, sums[:1])
    s1, nq = turned(q1, far, q2_b, [out])
    far = over_x(nq)
    ru, rd, a, b = stepped(u, d, True, [s1])
    v += [both([ru]), both([rd])]
    a, b = up(a), down(b)
    sums = late_part([3, 4], sums, False, [ru])
    out = collect(1, [s1, over_core(s1)], out, False, sums[:1])
    a, b = stepped(a, b, False, [out])
    v += [both([a, b])]
    s2, nq = turned(q2, far, q3_b, [a])
    far = over_x(nq)
    sums = late_part([5, 6], sums, False, [s2])
    out = collect(2, [s2, over_core(s2)], out, False, sums[:1])
    out = late_part([n - 1], sums, True, [], [p, out])[0]
    s3 = turned(q3, far, None, [out])[0]
    return collect(3, [s3, over_core(s3)], out, True)


def solution(mesh):
    n = mesh.shape["dp"]

    def on_device(tokens, weight):
        if mesh.shape["tensor"] == 4 and n == 8:
            return ring_form(n, tokens, weight)
        return gathered_form(tokens, weight)

    placed = (P(("dp", "tensor"), None), P("tensor", "dp"))
    return jax.shard_map(
        on_device, mesh=mesh, in_specs=placed, out_specs=P("dp", "tensor"), check_vma=False
    )
```

```python
import jax
import jax.numpy as jnp
from jax import lax
from jax.experimental import pallas as pl
from jax.experimental.pallas import tpu as pltpu
from jax.sharding import PartitionSpec as P

BF = jnp.bfloat16
F32 = jnp.float32
ANY = pl.BlockSpec(memory_space=pl.ANY)
HBM = pl.BlockSpec(memory_space=pltpu.HBM)
VMEM = pl.BlockSpec(memory_space=pltpu.VMEM)
LATE = 256


def contract_last(left, right):
    return lax.dot_general(left, right, (((1,), (1,)), ((), ())), preferred_element_type=F32)


def contract(left, right):
    return lax.dot_general(left, right, (((1,), (0,)), ((), ())), preferred_element_type=F32)


def gathered_form(tokens, weight):
    rows = lax.all_gather(weight, "dp", axis=1, tiled=True)
    toks = lax.all_gather(tokens, "tensor", axis=0, tiled=True)
    first = contract_last(toks, rows)
    part = contract(first.astype(BF), rows).astype(BF)
    second = lax.psum(part, "tensor")
    return (1.5 * first - 0.5 * contract_last(second, rows)).astype(BF)


def tiles(extent, step=256):
    return [slice(at, min(at + step, extent)) for at in range(0, extent, step)]


def call(body, ins, outs, flops, after=(), leave=False, scratch=(), out_left=False):
    flat, tree = jax.tree.flatten(ins)
    after = list(after)
    n_in, n_out = len(flat), len(outs)

    def kernel(*refs):
        given = jax.tree.unflatten(tree, refs[:n_in])
        rest = refs[n_in + len(after) :]
        body(given, rest[:n_out], *rest[n_out:])

    nbytes = sum(v.size * v.dtype.itemsize for v in flat)
    place = pltpu.HBM if leave else pltpu.VMEM
    flat = [pltpu.with_memory_space_constraint(v, place) for v in flat]
    return pl.pallas_call(
        kernel,
        out_shape=[pltpu.VMEM(*o) if isinstance(o, tuple) else o for o in outs],
        in_specs=[HBM if leave else VMEM] * n_in + [ANY] * len(after),
        out_specs=[ANY if out_left else VMEM] * n_out,
        scratch_shapes=[pltpu.SemaphoreType.DMA((n_out,))] if leave else list(scratch),
        compiler_params=pltpu.CompilerParams(vmem_limit_bytes=16 << 20),
        cost_estimate=pl.CostEstimate(flops=flops // 20, bytes_accessed=nbytes // 20, transcendentals=0),
    )(*flat, *after)


def bounds(pieces):
    ends = [0]
    for piece in pieces:
        ends.append(ends[-1] + piece.shape[0])
    return ends


def cuts(chunks):
    edges = sorted({e for pieces in chunks for e in bounds(pieces)})
    return [
        slice(a + t.start, a + t.stop) for a, b in zip(edges, edges[1:]) for t in tiles(b - a)
    ]


def at_rows(pieces, rows, cols=slice(None)):
    for ref, start in zip(pieces, bounds(pieces)):
        if start <= rows.start and rows.stop <= start + ref.shape[0]:
            return ref[rows.start - start : rows.stop - start, cols]


def add_dots(pairs, acc=None):
    for left, right in pairs:
        term = contract_last(left, right)
        acc = term if acc is None else acc + term
    return acc


def ring_form(n, tokens, weight):
    rows, width = weight.shape
    own = tokens.shape[0]
    count = 4 * own
    half = width // 2
    early = rows - LATE
    middle = early // 2
    steps = n // 2 - 1
    wide = 4 * LATE
    square = (count, width)
    offsets = [0] + [o for s in range(1, steps + 1) for o in (-s, s)] + [steps + 1]
    ring = list(range(0, n, 2)) + list(range(n - 1, 0, -2))

    def source(k):
        i = lax.axis_index("dp")
        place = jnp.where(lax.rem(i, 2) == 0, i // 2, n - 1 - i // 2)
        spot = lax.rem(place + offsets[k] + n, n)
        return jnp.where(spot < n // 2, 2 * spot, 2 * (n - 1 - spot) + 1)

    def side(mine):
        core = lax.rem(lax.axis_index("tensor"), 2)
        return core if mine else 1 - core

    def up(v):
        return lax.ppermute(v, "dp", [(ring[i], ring[(i + 1) % n]) for i in range(n)])

    def down(v):
        return lax.ppermute(v, "dp", [(ring[(i + 1) % n], ring[i]) for i in range(n)])

    def over_x(v):
        return lax.ppermute(v, "tensor", [(t, t ^ 2) for t in range(4)])

    def over_core(v):
        return lax.ppermute(v, "tensor", [(t, t ^ 1) for t in range(4)])

    def copy_from(row):
        def body(given, outs, sem):
            src = given[0].at[pl.ds(row, outs[0].shape[0]), :]
            copy = pltpu.make_async_copy(src, outs[0], sem.at[0])
            copy.start()
            copy.wait()

        return body

    def relay(given, outs):
        for ref, out in zip(given, outs):
            out[...] = ref[...]

    def relayed(arrays, after):
        return call(relay, arrays, [(a.shape, a.dtype) for a in arrays], 0, after)

    def split(given, outs):
        cut = outs[0].shape[0]
        outs[0][...] = given[0][:cut, :]
        outs[1][...] = given[1][cut:, :]

    def ends(u, d, after):
        h = u.shape[0] // 2
        return call(split, [u, d], [((h, width), BF), ((u.shape[0] - h, width), BF)], 0, after)

    def columns(k):
        return slice(k * width, (k + 1) * width)

    def halves(mine):
        return pl.ds(pl.multiple_of(side(mine) * half, half), half)

    def p_terms(tok, ks, chunks, acc_ref, put):
        for cut in cuts(chunks):
            pairs = [(tok[:, columns(k)], at_rows(c, cut)) for k, c in zip(ks, chunks)]
            put(cut, add_dots(pairs, None if acc_ref is None else acc_ref[:, cut]))

    def project(ks, acc, after=()):
        def body(given, outs):
            tok, chunks, acc_ref = given

            def put(cols, value):
                outs[0][:, cols] = value

            p_terms(tok, ks, chunks, acc_ref, put)

        outs = [((count, early), F32)]
        flops = 2 * count * early * width * len(ks)
        return call(body, (toks, [w[k] for k in ks], acc), outs, flops, after)[0]

    far = over_x(tokens)
    first = call(copy_from(0), [weight], [((early, width), BF)], 0, (), True)[0]
    u1, d1 = up(first), down(first)
    late = call(copy_from(early), [weight], [((LATE, width), BF)], 0, [u1, d1], True)[0]
    u2, d2 = up(u1), down(d1)
    u3, d3 = up(u2), down(d2)
    w = [[first], [u1], [d1], [u2], [d2], [u3], [d3]]

    def arrange(given, outs):
        core, x = side(True), lax.axis_index("tensor") // 2
        slots = [2 * x + core, 2 * (1 - x) + core, 2 * x + 1 - core, 2 * (1 - x) + 1 - core]
        for ref, slot in zip(given, slots):
            row = pl.multiple_of(slot * own, own)
            for k in range(n):
                src = pl.multiple_of(source(k) * width, width)
                outs[0][pl.ds(row, own), columns(k)] = ref[:, pl.ds(src, width)]

    toks = call(
        arrange,
        [tokens, far, over_core(tokens), over_core(far)],
        [((count, n * width), BF)],
        0,
    )[0]
    acc = project(list(range(n - 3)), None)
    late_far = over_x(late)
    a, b = ends(u3, d3, [acc, late_far])
    w.append([up(a), down(b)])
    acc = project([n - 3, n - 2], acc)

    def q_terms(p_ref, chunk, cols):
        total = None
        for ref, start in zip(chunk, bounds(chunk)):
            term = contract(p_ref[:, start : start + ref.shape[0]], ref[:, cols])
            total = term if total is None else total + term
        return total

    sizes = [u * half // 2 for u in (4,5,5,2)]
    starts = [sum(sizes[:g]) for g in range(len(sizes))]

    def spots(g):
        found = []
        for k in range(n):
            lo = max(starts[g], k * half)
            hi = min(starts[g] + sizes[g], (k + 1) * half)
            if lo < hi:
                found.append((k, slice(lo - starts[g], hi - starts[g]), lo - k * half, hi - lo))
        return found

    def block_columns(mine, offset, size):
        return pl.ds(pl.multiple_of(side(mine) * half + offset, 128), size)

    def put_q(p_ref, g, chunks, mine, out):
        for (_, here, offset, size), chunk in zip(spots(g), chunks):
            q = q_terms(p_ref, chunk, block_columns(mine, offset, size))
            out[:, here] = q.astype(out.dtype)

    def part_of_w(g):
        return [w[k] for k, *_ in spots(g)]

    def first_give(given, outs):
        tok, last, acc_ref, chunks = given

        def put(cols, value):
            outs[0][:, cols] = value
            outs[1][:, cols] = value.astype(BF)

        p_terms(tok, [n - 1], [last], acc_ref, put)
        put_q(outs[1], 0, chunks, False, outs[2])

    def q_flops(g):
        return 2 * count * early * sizes[g]

    p, p_b, give = call(
        first_give,
        (toks, w[-1], acc, part_of_w(0)),
        [((count, early), F32), ((count, early), BF), ((count, sizes[0]), BF)],
        2 * q_flops(0),
    )

    def q_part(gs, mine, dtype, after=()):
        def body(given, outs):
            start = 0
            for at, (g, chunks) in enumerate(zip(gs, given[1])):
                out = outs[at] if mine else outs[0].at[:, start : start + sizes[g]]
                put_q(given[0], g, chunks, mine, out)
                start += sizes[g]

        outs = [((count, sizes[g]), dtype) for g in gs]
        if not mine:
            outs = [((count, sum(sizes[g] for g in gs)), dtype)]
        ins = (p_b, [part_of_w(g) for g in gs])
        return call(body, ins, outs, sum(q_flops(g) for g in gs), after)

    def add_two(given, outs):
        keep, got = given
        start = 0
        for at, a in enumerate(keep):
            q = a[...] + got[:, start : start + a.shape[1]].astype(F32)
            outs[2 * at][...] = q
            outs[2 * at + 1][...] = q.astype(BF)
            start += a.shape[1]

    def q_sum(keep, give):
        outs = [((count, k.shape[1]), dtype) for k in keep for dtype in (F32, BF)]
        return call(add_two, (keep, over_core(give)), outs, 0)

    keep = q_part([0], True, F32)
    give1 = q_part([1], False, BF, keep)[0]
    q0, q0_b = q_sum(keep, give)
    keep1 = q_part([1], True, F32, [q0_b])
    q1, q1_b = q_sum(keep1, give1)
    keep = q_part([2, 3], True, F32, [q0_b])
    give = q_part([2, 3], False, BF, keep)[0]
    q2, q2_b, q3, q3_b = q_sum(keep, give)

    def late_part(ks, accs, final, after=(), more=None):
        def body(given, outs, *scratch):
            tok, lates, earlies, acc_refs, more = given
            p_out, g_out = scratch if final else outs

            def old(which, rows, cols):
                return None if accs is None else acc_refs[which][rows, cols]

            flat = [[m[0], m[1], o[0], o[1]] if len(m) == 2 else [m[0], o[0]] for m, o in lates]
            sets = [slice(j * LATE, (j + 1) * LATE) for j in range(4)]
            for cols in sets:
                pairs = [(tok[:, columns(k)], at_rows(f, cols)) for k, f in zip(ks, flat)]
                value = add_dots(pairs, old(0, slice(None), cols))
                p_out[:, cols] = value.astype(p_out.dtype)
                if final and cols.start == 0:
                    p_own = value
            for here in sets:
                for cols in cuts(earlies):
                    pairs = [(at_rows(f, here), at_rows(e, cols)) for f, e in zip(flat, earlies)]
                    g_out[here, cols] = add_dots(pairs, old(1, here, cols)).astype(g_out.dtype)
                cols = slice(early, rows)
                pairs = [(at_rows(f, here), at_rows(f, sets[0])) for f in flat]
                g_out[here, cols] = add_dots(pairs, old(1, here, cols)).astype(g_out.dtype)
            if final:
                p_ref, q_ref = more
                for cols in tiles(early) + [slice(early, rows)]:
                    p_val = p_ref[:, cols] if cols.start < early else p_own
                    term = q_ref[:, cols] + contract(p_out[...], g_out[:, cols])
                    outs[0][:, cols] = 1.5 * p_val - 0.5 * term

        if final:
            outs = [((count, rows), F32)]
            scratch = [pltpu.VMEM((count, wide), BF), pltpu.VMEM((wide, rows), BF)]
        else:
            outs = [((count, wide), F32), ((wide, rows), F32)]
            scratch = []
        flops = 2 * wide * (count + rows) * width * len(ks)
        ins = (toks, [v[k] for k in ks], [w[k] for k in ks], accs, more)
        return call(body, ins, outs, flops, after, False, scratch)

    def collect(g, sides, out, final, after=()):
        def body(given, outs, *scratch):
            side_refs, chunks, base_ref = given
            copies = []
            for cols in cuts([e for e, _ in chunks]) + [slice(early, rows)]:
                term = None if out is None or final else base_ref[:, cols]
                for (_, here, offset, size), (early_rows, late_rows) in zip(spots(g), chunks):
                    for ref, mine in zip(side_refs, (True, False)):
                        left = ref[:, here]
                        block_cols = block_columns(mine, offset, size)
                        if cols.start < early:
                            right = at_rows(early_rows, cols, block_cols)
                        else:
                            right = late_rows[0][0][:LATE, block_cols]
                        term = add_dots([(left, right)], term)
                if final:
                    term = base_ref[:, cols] - 0.5 * term
                if not final:
                    outs[0][:, cols] = term
                    continue
                buf, sem = scratch
                buf[:, cols] = term.astype(BF)
                copies.append(
                    pltpu.make_async_copy(buf.at[:, cols], outs[0].at[:, cols], sem.at[len(copies)])
                )
                copies[-1].start()
            for copy in copies:
                copy.wait()

        outs = [jax.ShapeDtypeStruct((count, rows), BF) if final else ((count, rows), F32)]
        ins = (sides, [(w[k], v[k]) for k, *_ in spots(g)], out)
        scratch = ()
        if final:
            scratch = [pltpu.VMEM((count, rows), BF), pltpu.SemaphoreType.DMA((n,))]
        flops = 4 * count * rows * sizes[g]
        return call(body, ins, outs, flops, after, False, scratch, final)[0]

    def join(given, outs):
        outs[0][:LATE, :] = given[0][...]
        outs[0][LATE:, :] = given[1][...]

    def turn(given, outs):
        q_ref, far_ref, next_ref = given
        outs[0][...] = (q_ref[...] + far_ref[...].astype(F32)).astype(BF)
        if next_ref is not None:
            outs[1][...] = next_ref[...]

    def turned(q, far, next_q, after):
        outs = [(q.shape, BF)] + ([] if next_q is None else [(next_q.shape, BF)])
        return call(turn, (q, far, next_q), outs, 0, after)

    def step(given, outs):
        relay(given, outs[:2])
        if len(outs) > 2:
            split(given, outs[2:])

    def stepped(u, d, last, after):
        outs = [(u.shape, BF), (d.shape, BF)] + ([((LATE, width), BF)] * 2 if last else [])
        return call(step, [u, d], outs, 0, after)

    def both(pieces):
        return (pieces, [over_core(c) for c in pieces])

    tall = 2 * LATE
    block = call(join, [late, late_far], [((tall, width), BF)], 0, [p_b])[0]
    v = [both([block])]
    u, d = up(block), down(block)
    far = over_x(q0_b)
    sums = late_part([0], None, False, [q0_b])
    ru, rd = stepped(u, d, False, [sums[0], give, keep1[0]])
    v += [both([ru]), both([rd])]
    u, d = up(ru), down(rd)
    s0, nq = turned(q0, far, q1_b, [ru, q2_b])
    far = over_x(nq)
    ru, rd = stepped(u, d, False, [s0])
    v += [both([ru]), both([rd])]
    u, d = up(ru), down(rd)
    sums = late_part([1, 2], sums, False, [ru])
    out = collect(0, [s0, over_core(s0)], None, False, sums[:1])
    s1, nq = turned(q1, far, q2_b, [out])
    far = over_x(nq)
    ru, rd, a, b = stepped(u, d, True, [s1])
    v += [both([ru]), both([rd])]
    a, b = up(a), down(b)
    sums = late_part([3, 4], sums, False, [ru])
    out = collect(1, [s1, over_core(s1)], out, False, sums[:1])
    a, b = stepped(a, b, False, [out])
    v += [both([a, b])]
    s2, nq = turned(q2, far, q3_b, [a])
    far = over_x(nq)
    sums = late_part([5, 6], sums, False, [s2])
    out = collect(2, [s2, over_core(s2)], out, False, sums[:1])
    out = late_part([n - 1], sums, True, [], [p, out])[0]
    s3 = turned(q3, far, None, [out])[0]
    return collect(3, [s3, over_core(s3)], out, True)


def solution(mesh):
    n = mesh.shape["dp"]

    def on_device(tokens, weight):
        if mesh.shape["tensor"] == 4 and n == 8:
            return ring_form(n, tokens, weight)
        return gathered_form(tokens, weight)

    placed = (P(("dp", "tensor"), None), P("tensor", "dp"))
    return jax.shard_map(
        on_device, mesh=mesh, in_specs=placed, out_specs=P("dp", "tensor"), check_vma=False
    )
```

```python
import jax
import jax.numpy as jnp
from jax import lax
from jax.experimental import pallas as pl
from jax.experimental.pallas import tpu as pltpu
from jax.sharding import PartitionSpec as P

BF = jnp.bfloat16
F32 = jnp.float32
ANY = pl.BlockSpec(memory_space=pl.ANY)
HBM = pl.BlockSpec(memory_space=pltpu.HBM)
VMEM = pl.BlockSpec(memory_space=pltpu.VMEM)
LATE = 256


def contract_last(left, right):
    return lax.dot_general(left, right, (((1,), (1,)), ((), ())), preferred_element_type=F32)


def contract(left, right):
    return lax.dot_general(left, right, (((1,), (0,)), ((), ())), preferred_element_type=F32)


def gathered_form(tokens, weight):
    rows = lax.all_gather(weight, "dp", axis=1, tiled=True)
    toks = lax.all_gather(tokens, "tensor", axis=0, tiled=True)
    first = contract_last(toks, rows)
    part = contract(first.astype(BF), rows).astype(BF)
    second = lax.psum(part, "tensor")
    return (1.5 * first - 0.5 * contract_last(second, rows)).astype(BF)


def tiles(extent, step=256):
    return [slice(at, min(at + step, extent)) for at in range(0, extent, step)]


def call(body, ins, outs, flops, after=(), leave=False, scratch=()):
    flat, tree = jax.tree.flatten(ins)
    after = list(after)
    n_in, n_out = len(flat), len(outs)

    def kernel(*refs):
        given = jax.tree.unflatten(tree, refs[:n_in])
        rest = refs[n_in + len(after) :]
        body(given, rest[:n_out], *rest[n_out:])

    nbytes = sum(v.size * v.dtype.itemsize for v in flat)
    place = pltpu.HBM if leave else pltpu.VMEM
    flat = [pltpu.with_memory_space_constraint(v, place) for v in flat]
    return pl.pallas_call(
        kernel,
        out_shape=[pltpu.VMEM(*o) if isinstance(o, tuple) else o for o in outs],
        in_specs=[HBM if leave else VMEM] * n_in + [ANY] * len(after),
        out_specs=[VMEM] * n_out,
        scratch_shapes=[pltpu.SemaphoreType.DMA((n_out,))] if leave else list(scratch),
        compiler_params=pltpu.CompilerParams(vmem_limit_bytes=16 << 20),
        cost_estimate=pl.CostEstimate(flops=flops // 20, bytes_accessed=nbytes // 20, transcendentals=0),
    )(*flat, *after)


def bounds(pieces):
    ends = [0]
    for piece in pieces:
        ends.append(ends[-1] + piece.shape[0])
    return ends


def cuts(chunks):
    edges = sorted({e for pieces in chunks for e in bounds(pieces)})
    return [
        slice(a + t.start, a + t.stop) for a, b in zip(edges, edges[1:]) for t in tiles(b - a)
    ]


def at_rows(pieces, rows, cols=slice(None)):
    for ref, start in zip(pieces, bounds(pieces)):
        if start <= rows.start and rows.stop <= start + ref.shape[0]:
            return ref[rows.start - start : rows.stop - start, cols]


def add_dots(pairs, acc=None):
    for left, right in pairs:
        term = contract_last(left, right)
        acc = term if acc is None else acc + term
    return acc


def ring_form(n, tokens, weight):
    rows, width = weight.shape
    own = tokens.shape[0]
    count = 4 * own
    half = width // 2
    early = rows - LATE
    middle = early // 2
    steps = n // 2 - 1
    wide = 4 * LATE
    square = (count, width)
    offsets = [0] + [o for s in range(1, steps + 1) for o in (-s, s)] + [steps + 1]
    ring = list(range(0, n, 2)) + list(range(n - 1, 0, -2))

    def source(k):
        i = lax.axis_index("dp")
        place = jnp.where(lax.rem(i, 2) == 0, i // 2, n - 1 - i // 2)
        spot = lax.rem(place + offsets[k] + n, n)
        return jnp.where(spot < n // 2, 2 * spot, 2 * (n - 1 - spot) + 1)

    def side(mine):
        core = lax.rem(lax.axis_index("tensor"), 2)
        return core if mine else 1 - core

    def up(v):
        return lax.ppermute(v, "dp", [(ring[i], ring[(i + 1) % n]) for i in range(n)])

    def down(v):
        return lax.ppermute(v, "dp", [(ring[(i + 1) % n], ring[i]) for i in range(n)])

    def over_x(v):
        return lax.ppermute(v, "tensor", [(t, t ^ 2) for t in range(4)])

    def over_core(v):
        return lax.ppermute(v, "tensor", [(t, t ^ 1) for t in range(4)])

    def copy_from(row):
        def body(given, outs, sem):
            src = given[0].at[pl.ds(row, outs[0].shape[0]), :]
            copy = pltpu.make_async_copy(src, outs[0], sem.at[0])
            copy.start()
            copy.wait()

        return body

    def relay(given, outs):
        for ref, out in zip(given, outs):
            out[...] = ref[...]

    def relayed(arrays, after):
        return call(relay, arrays, [(a.shape, a.dtype) for a in arrays], 0, after)

    def split(given, outs):
        cut = outs[0].shape[0]
        outs[0][...] = given[0][:cut, :]
        outs[1][...] = given[1][cut:, :]

    def ends(u, d, after):
        h = u.shape[0] // 2
        return call(split, [u, d], [((h, width), BF), ((u.shape[0] - h, width), BF)], 0, after)

    def columns(k):
        return slice(k * width, (k + 1) * width)

    def halves(mine):
        return pl.ds(pl.multiple_of(side(mine) * half, half), half)

    def p_terms(tok, ks, chunks, acc_ref, put):
        for cut in cuts(chunks):
            pairs = [(tok[:, columns(k)], at_rows(c, cut)) for k, c in zip(ks, chunks)]
            put(cut, add_dots(pairs, None if acc_ref is None else acc_ref[:, cut]))

    def project(ks, acc, after=()):
        def body(given, outs):
            tok, chunks, acc_ref = given

            def put(cols, value):
                outs[0][:, cols] = value

            p_terms(tok, ks, chunks, acc_ref, put)

        outs = [((count, early), F32)]
        flops = 2 * count * early * width * len(ks)
        return call(body, (toks, [w[k] for k in ks], acc), outs, flops, after)[0]

    far = over_x(tokens)
    first = call(copy_from(0), [weight], [((early, width), BF)], 0, (), True)[0]
    u1, d1 = up(first), down(first)
    late = call(copy_from(early), [weight], [((LATE, width), BF)], 0, [u1, d1], True)[0]
    u2, d2 = up(u1), down(d1)
    u3, d3 = up(u2), down(d2)
    w = [[first], [u1], [d1], [u2], [d2], [u3], [d3]]

    def arrange(given, outs):
        core, x = side(True), lax.axis_index("tensor") // 2
        slots = [2 * x + core, 2 * (1 - x) + core, 2 * x + 1 - core, 2 * (1 - x) + 1 - core]
        for ref, slot in zip(given, slots):
            row = pl.multiple_of(slot * own, own)
            for k in range(n):
                src = pl.multiple_of(source(k) * width, width)
                outs[0][pl.ds(row, own), columns(k)] = ref[:, pl.ds(src, width)]

    toks = call(
        arrange,
        [tokens, far, over_core(tokens), over_core(far)],
        [((count, n * width), BF)],
        0,
    )[0]
    acc = project(list(range(n - 3)), None)
    late_far = over_x(late)
    a, b = ends(u3, d3, [acc, late_far])
    w.append([up(a), down(b)])
    acc = project([n - 3, n - 2], acc)

    def q_terms(p_ref, chunk, cols):
        total = None
        for ref, start in zip(chunk, bounds(chunk)):
            term = contract(p_ref[:, start : start + ref.shape[0]], ref[:, cols])
            total = term if total is None else total + term
        return total

    sizes = [u * half // 2 for u in (4,5,5,2)]
    starts = [sum(sizes[:g]) for g in range(len(sizes))]

    def spots(g):
        found = []
        for k in range(n):
            lo = max(starts[g], k * half)
            hi = min(starts[g] + sizes[g], (k + 1) * half)
            if lo < hi:
                found.append((k, slice(lo - starts[g], hi - starts[g]), lo - k * half, hi - lo))
        return found

    def block_columns(mine, offset, size):
        return pl.ds(pl.multiple_of(side(mine) * half + offset, 128), size)

    def put_q(p_ref, g, chunks, mine, out):
        for (_, here, offset, size), chunk in zip(spots(g), chunks):
            q = q_terms(p_ref, chunk, block_columns(mine, offset, size))
            out[:, here] = q.astype(out.dtype)

    def part_of_w(g):
        return [w[k] for k, *_ in spots(g)]

    def first_give(given, outs):
        tok, last, acc_ref, chunks = given

        def put(cols, value):
            outs[0][:, cols] = value
            outs[1][:, cols] = value.astype(BF)

        p_terms(tok, [n - 1], [last], acc_ref, put)
        put_q(outs[1], 0, chunks, False, outs[2])

    def q_flops(g):
        return 2 * count * early * sizes[g]

    p, p_b, give = call(
        first_give,
        (toks, w[-1], acc, part_of_w(0)),
        [((count, early), F32), ((count, early), BF), ((count, sizes[0]), BF)],
        2 * q_flops(0),
    )

    def q_part(gs, mine, dtype, after=()):
        def body(given, outs):
            start = 0
            for at, (g, chunks) in enumerate(zip(gs, given[1])):
                out = outs[at] if mine else outs[0].at[:, start : start + sizes[g]]
                put_q(given[0], g, chunks, mine, out)
                start += sizes[g]

        outs = [((count, sizes[g]), dtype) for g in gs]
        if not mine:
            outs = [((count, sum(sizes[g] for g in gs)), dtype)]
        ins = (p_b, [part_of_w(g) for g in gs])
        return call(body, ins, outs, sum(q_flops(g) for g in gs), after)

    def add_two(given, outs):
        keep, got = given
        start = 0
        for at, a in enumerate(keep):
            q = a[...] + got[:, start : start + a.shape[1]].astype(F32)
            outs[2 * at][...] = q
            outs[2 * at + 1][...] = q.astype(BF)
            start += a.shape[1]

    def q_sum(keep, give):
        outs = [((count, k.shape[1]), dtype) for k in keep for dtype in (F32, BF)]
        return call(add_two, (keep, over_core(give)), outs, 0)

    keep = q_part([0], True, F32)
    give1 = q_part([1], False, BF, keep)[0]
    q0, q0_b = q_sum(keep, give)
    keep = q_part([1], True, F32, [q0_b])
    q1, q1_b = q_sum(keep, give1)
    keep = q_part([2, 3], True, F32, [q0_b])
    give = q_part([2, 3], False, BF, keep)[0]
    q2, q2_b, q3, q3_b = q_sum(keep, give)

    def late_part(ks, accs, final, after=(), more=None):
        def body(given, outs, *scratch):
            tok, lates, earlies, acc_refs, more = given
            p_out, g_out = scratch if final else outs

            def old(which, rows, cols):
                return None if accs is None else acc_refs[which][rows, cols]

            flat = [[m[0], m[1], o[0], o[1]] if len(m) == 2 else [m[0], o[0]] for m, o in lates]
            sets = [slice(j * LATE, (j + 1) * LATE) for j in range(4)]
            for cols in sets:
                pairs = [(tok[:, columns(k)], at_rows(f, cols)) for k, f in zip(ks, flat)]
                value = add_dots(pairs, old(0, slice(None), cols))
                p_out[:, cols] = value.astype(p_out.dtype)
                if final and cols.start == 0:
                    p_own = value
            for here in sets:
                for cols in cuts(earlies):
                    pairs = [(at_rows(f, here), at_rows(e, cols)) for f, e in zip(flat, earlies)]
                    g_out[here, cols] = add_dots(pairs, old(1, here, cols)).astype(g_out.dtype)
                cols = slice(early, rows)
                pairs = [(at_rows(f, here), at_rows(f, sets[0])) for f in flat]
                g_out[here, cols] = add_dots(pairs, old(1, here, cols)).astype(g_out.dtype)
            if final:
                p_ref, q_ref = more
                for cols in tiles(early) + [slice(early, rows)]:
                    p_val = p_ref[:, cols] if cols.start < early else p_own
                    term = q_ref[:, cols] + contract(p_out[...], g_out[:, cols])
                    outs[0][:, cols] = 1.5 * p_val - 0.5 * term

        if final:
            outs = [((count, rows), F32)]
            scratch = [pltpu.VMEM((count, wide), BF), pltpu.VMEM((wide, rows), BF)]
        else:
            outs = [((count, wide), F32), ((wide, rows), F32)]
            scratch = []
        flops = 2 * wide * (count + rows) * width * len(ks)
        ins = (toks, [v[k] for k in ks], [w[k] for k in ks], accs, more)
        return call(body, ins, outs, flops, after, False, scratch)

    def collect(g, sides, out, final, after=()):
        def body(given, outs):
            side_refs, chunks, base_ref = given
            for cols in cuts([e for e, _ in chunks]) + [slice(early, rows)]:
                term = None if out is None or final else base_ref[:, cols]
                for (_, here, offset, size), (early_rows, late_rows) in zip(spots(g), chunks):
                    for ref, mine in zip(side_refs, (True, False)):
                        left = ref[:, here]
                        block_cols = block_columns(mine, offset, size)
                        if cols.start < early:
                            right = at_rows(early_rows, cols, block_cols)
                        else:
                            right = late_rows[0][0][:LATE, block_cols]
                        term = add_dots([(left, right)], term)
                if final:
                    term = base_ref[:, cols] - 0.5 * term
                outs[0][:, cols] = term.astype(outs[0].dtype)

        outs = [jax.ShapeDtypeStruct((count, rows), BF) if final else ((count, rows), F32)]
        ins = (sides, [(w[k], v[k]) for k, *_ in spots(g)], out)
        return call(body, ins, outs, 4 * count * rows * sizes[g], after)[0]

    def join(given, outs):
        outs[0][:LATE, :] = given[0][...]
        outs[0][LATE:, :] = given[1][...]

    def turn(given, outs):
        q_ref, far_ref, next_ref = given
        outs[0][...] = (q_ref[...] + far_ref[...].astype(F32)).astype(BF)
        if next_ref is not None:
            outs[1][...] = next_ref[...]

    def turned(q, far, next_q, after):
        outs = [(q.shape, BF)] + ([] if next_q is None else [(next_q.shape, BF)])
        return call(turn, (q, far, next_q), outs, 0, after)

    def step(given, outs):
        relay(given, outs[:2])
        if len(outs) > 2:
            split(given, outs[2:])

    def stepped(u, d, last, after):
        outs = [(u.shape, BF), (d.shape, BF)] + ([((LATE, width), BF)] * 2 if last else [])
        return call(step, [u, d], outs, 0, after)

    def both(pieces):
        return (pieces, [over_core(c) for c in pieces])

    tall = 2 * LATE
    block = call(join, [late, late_far], [((tall, width), BF)], 0, [p_b])[0]
    v = [both([block])]
    u, d = up(block), down(block)
    far = over_x(q0_b)
    sums = late_part([0], None, False, [q0_b])
    ru, rd = stepped(u, d, False, [sums[0], give])
    v += [both([ru]), both([rd])]
    u, d = up(ru), down(rd)
    s0, nq = turned(q0, far, q1_b, [ru, q2_b])
    far = over_x(nq)
    ru, rd = stepped(u, d, False, [s0])
    v += [both([ru]), both([rd])]
    u, d = up(ru), down(rd)
    sums = late_part([1, 2], sums, False, [ru])
    out = collect(0, [s0, over_core(s0)], None, False, sums[:1])
    s1, nq = turned(q1, far, q2_b, [out])
    far = over_x(nq)
    ru, rd, a, b = stepped(u, d, True, [s1])
    v += [both([ru]), both([rd])]
    a, b = up(a), down(b)
    sums = late_part([3, 4], sums, False, [ru])
    out = collect(1, [s1, over_core(s1)], out, False, sums[:1])
    a, b = stepped(a, b, False, [out])
    v += [both([a, b])]
    s2, nq = turned(q2, far, q3_b, [a])
    far = over_x(nq)
    sums = late_part([5, 6], sums, False, [s2])
    out = collect(2, [s2, over_core(s2)], out, False, sums[:1])
    s3 = turned(q3, far, None, [out])[0]
    out = late_part([n - 1], sums, True, [s3], [p, out])[0]
    return collect(3, [s3, over_core(s3)], out, True)


def solution(mesh):
    n = mesh.shape["dp"]

    def on_device(tokens, weight):
        if mesh.shape["tensor"] == 4 and n == 8:
            return ring_form(n, tokens, weight)
        return gathered_form(tokens, weight)

    placed = (P(("dp", "tensor"), None), P("tensor", "dp"))
    return jax.shard_map(
        on_device, mesh=mesh, in_specs=placed, out_specs=P("dp", "tensor"), check_vma=False
    )
```
